256 devices in a mesh: pts: 64 (over y, z_lo, x), prb: 4 (over z_hi, core).
Axes of the slice: x: 4, y: 4, z: 8 (z_hi: 2, z_lo: 4; z = z_hi * 4 + z_lo), core: 2. Of those that a mesh axis runs over, the one named last changes fastest.
Arguments:
- probe_vectors: bfloat16 [2, 32, 524288], P(None, 'prb', 'pts'), may hold values from -6 to 6
- factors: bfloat16 [6, 2, 524288, 128], P(None, None, ('pts', 'prb')), may hold values from -0.375 to 0.375
- row_orders: int32 [6, 2048], replicated, may hold values from 0 to 2047, each once within a row
Outputs:
- applied: bfloat16 [2, 32, 524288], P(None, 'prb', 'pts')
The draws below stay inside these ranges and needn't reach their ends.
All inputs are finite; a program needn't handle non-finite values.
Results may differ from the reference program's by a relative error of at most 0.013.
Values may be sent and summed in bfloat16 or wider, within the bound.
No kernel may reach another device: no remote copies, remote signals or barrier semaphores. Data moves between devices by JAX's collectives and lax.ppermute only.
A program may use at most 128 MiB of HBM per device.

```python
import jax
import jax.numpy as jnp
from jax import lax

PROBES = 32
RANK = 64
LEVELS = 6
ROWS_SUB = 2048
POINTS = 524288
N_PTS = 64
N_PRB = 4


def shard_levels(rng, extent, split, least, largest):
    level, own = 1.0, jax.random.fold_in(rng, 6)
    for dim, blocks in split:
        draws = jnp.exp(jax.random.uniform(jax.random.fold_in(own, dim), (blocks,), jnp.float32, least / len(split), largest / len(split)))
        level = level * jnp.repeat(draws, extent[dim] // blocks).reshape([-1 if axis == dim else 1 for axis in range(len(extent))])
    return level


def noise(stream_key, extent, spread, limit, split=(), held_as=jnp.bfloat16):
    drawn = jax.random.normal(stream_key, extent, jnp.float32) * spread
    if len(split) > 0:
        drawn = shard_levels(stream_key, extent, split, -0.22, 0.18) * drawn
    return jnp.clip(drawn, min=-limit, max=limit).astype(held_as)


def setup_inputs(seed: int = 0) -> dict:
    key_of = jax.random.split(jax.random.key(seed), 4)
    probe_vectors = noise(key_of[0], (2, PROBES, POINTS), 1.0, 6.0, ((1, 4), (2, 64)))
    factors = noise(key_of[1], (LEVELS, 2, POINTS, 2 * RANK), (4 * RANK) ** -0.5, 0.375, ((2, 256),))
    row_orders = jax.vmap(lambda own: jax.random.permutation(own, ROWS_SUB))(jax.random.split(key_of[2], LEVELS)).reshape((LEVELS, ROWS_SUB)).astype(jnp.int32)
    return dict(probe_vectors=probe_vectors, factors=factors, row_orders=row_orders)


def one_group(pair):
    joined, blocks = pair
    joined = joined.astype(jnp.float32)
    blocks = blocks.astype(jnp.float32)
    real_part = jnp.einsum('pqki,qkoi->pqko', joined[0], blocks[0]) - jnp.einsum('pqki,qkoi->pqko', joined[1], blocks[1])
    imag_part = jnp.einsum('pqki,qkoi->pqko', joined[1], blocks[0]) + jnp.einsum('pqki,qkoi->pqko', joined[0], blocks[1])
    return jnp.stack([real_part, imag_part]).astype(jnp.bfloat16)


def reference(probe_vectors, factors, row_orders):
    block = 2 * RANK
    nblocks = ROWS_SUB // block
    half_rows = ROWS_SUB // 2
    bit_count = int(N_PTS).bit_length() - 1
    current = probe_vectors.reshape(2, PROBES, N_PTS, N_PRB, ROWS_SUB)
    device_ids = jnp.arange(N_PTS, dtype=jnp.int32)
    for level_index in range(LEVELS):
        bit = level_index % bit_count
        permuted = jnp.take(current, row_orders[level_index], axis=4)
        partner = jnp.bitwise_xor(device_ids, 1 << bit)
        partner_rows = jnp.take(permuted, partner, axis=2)
        upper = ((device_ids // (1 << bit)) % 2 == 1)[None, None, :, None, None]
        kept_rows = jnp.where(upper, permuted[..., half_rows:], permuted[..., :half_rows])
        got_rows = jnp.where(upper, partner_rows[..., half_rows:], partner_rows[..., :half_rows])
        joined = jnp.concatenate([kept_rows.reshape(2, PROBES, N_PTS, N_PRB, nblocks, RANK),
                                  got_rows.reshape(2, PROBES, N_PTS, N_PRB, nblocks, RANK)], axis=5)
        layer = factors[level_index].reshape(2, N_PTS, N_PRB, nblocks, block, block)
        result = lax.map(one_group, (jnp.moveaxis(joined, 2, 0), jnp.moveaxis(layer, 1, 0)))
        current = jnp.moveaxis(result, 0, 2).reshape(2, PROBES, N_PTS, N_PRB, ROWS_SUB)
    pieces = current.reshape(2, PROBES, N_PTS, N_PRB, N_PTS, ROWS_SUB // N_PTS)
    pieces = jnp.transpose(pieces, (0, 1, 4, 5, 3, 2))
    return pieces.reshape(2, PROBES, N_PTS * N_PRB * ROWS_SUB)
```

```python
import functools

import jax
import jax.numpy as jnp
from jax import lax
from jax.experimental import pallas as pl
from jax.experimental.pallas import tpu as pltpu
from jax.sharding import Mesh
from jax.sharding import PartitionSpec as P

RANK = 64
BLOCK = 2 * RANK
LEVELS = 6
LANES = 128
TILE = 16
BF16 = jnp.bfloat16
F32 = jnp.float32

ALONG_LANES = lax.GatherDimensionNumbers(
    offset_dims=(),
    collapsed_slice_dims=(1,),
    start_index_map=(1,),
    operand_batching_dims=(0,),
    start_indices_batching_dims=(0,),
)
BY_LAST = (((1,), (1,)), ((), ()))


def take_lanes(value, lanes):
    return lax.gather(
        value, lanes[..., None], ALONG_LANES, (1, 1), mode=lax.GatherScatterMode.PROMISE_IN_BOUNDS
    )


def gather_half(sources, order_ref, level, start, targets):
    half = order_ref.shape[1] // 2
    for t in range(half // LANES):
        columns = pl.ds(pl.multiple_of(start + t * LANES, LANES), LANES)
        index = jnp.broadcast_to(order_ref[level : level + 1, columns], (TILE, LANES))
        lane = (index % LANES).astype(jnp.int16)
        which = (index // LANES).astype(jnp.int16)
        picked = [None] * len(sources)
        for s in range(2 * half // LANES):
            here = which == jnp.int16(s)
            for g, source in enumerate(sources):
                value = take_lanes(source(s), lane)
                picked[g] = value if s == 0 else jnp.where(here, value, picked[g])
        for g, (ref, row) in enumerate(targets):
            ref[row : row + TILE, t * LANES : (t + 1) * LANES] = picked[g]


def turned(tile):
    wide = tile.astype(F32)
    return jnp.concatenate([-wide[8:], wide[:8]], 0).astype(BF16)


def joined_blocks(kept, got):
    pairs = [(k, g, turned(k), turned(g)) for k, g in zip(kept, got)]
    for m in range(kept[0].shape[1] // LANES):
        for side in range(2):
            at = slice(m * LANES + side * RANK, m * LANES + (side + 1) * RANK)
            yield 2 * m + side, [
                jnp.concatenate([k[:, at], g[:, at], tk[:, at], tg[:, at]], 1)
                for k, g, tk, tg in pairs
            ]


def block_factors(f_refs, k):
    return jnp.concatenate([ref[k * BLOCK : (k + 1) * BLOCK, :] for ref in f_refs], 1)


def upper_half(bit):
    return lax.axis_index("pts") // (1 << bit) % 2


def fetch_kernel(f_hbm, *refs):
    outs, sems = refs[:-1], refs[-1]
    copies = [
        pltpu.make_async_copy(f_hbm.at[i // 2, i % 2], out, sems.at[i]) for i, out in enumerate(outs)
    ]
    for copy in copies:
        copy.start()
    for copy in copies:
        copy.wait()


def start_kernel(x_ref, order_ref, *outs):
    upper = upper_half(0)
    zhi, core = lax.axis_index("h"), lax.axis_index("c")
    rows = order_ref.shape[1]
    half = rows // 2

    def columns(qh, qc):
        def column(s):
            at = pl.multiple_of((qh * 2 + qc) * rows + s * LANES, LANES)
            return jnp.concatenate(
                [x_ref[0, :, pl.ds(at, LANES)].astype(F32), x_ref[1, :, pl.ds(at, LANES)].astype(F32)], 0
            ).astype(BF16)

        return [column(s) for s in range(rows // LANES)]

    groups = [
        columns(zhi, core), columns(1 - zhi, core), columns(zhi, 1 - core), columns(1 - zhi, 1 - core),
    ]
    sources = [lambda s, g=g: g[s] for g in groups]
    gather_half(sources, order_ref, 0, upper * half, [(out, 0) for out in outs])
    gather_half(sources, order_ref, 0, (1 - upper) * half, [(out, TILE) for out in outs])


def tiles_of(refs, rows):
    if len(refs) == 4:
        tiles = [ref[row : row + TILE, :] for ref, row in zip(refs, rows)]
    else:
        tiles = [ref[row : row + TILE, :] for ref in refs for row in (0, TILE)]
    return tiles[:2], tiles[2:]


def gather_sent_kernel(core_ref, ref, sent_out):
    sent_out[:TILE, :] = core_ref[TILE:, :]
    sent_out[TILE:, :] = ref[TILE:, :]


def level_kernel(level, at, *refs):
    operands, (*f_refs, order_ref, sent_out, current) = refs[:-5], refs[-5:]
    kept, got = tiles_of(operands, at)
    for k, lhs in joined_blocks(kept, got):
        out = lax.dot_general(
            jnp.concatenate(lhs, 0), block_factors(f_refs, k), BY_LAST, preferred_element_type=F32
        )
        current[:, k * BLOCK : (k + 1) * BLOCK] = out.astype(BF16)
    half = order_ref.shape[1] // 2
    upper = upper_half(level + 1)
    count = len(kept)
    sources = [
        (lambda s, g=g: current[g * TILE : (g + 1) * TILE, s * LANES : (s + 1) * LANES])
        for g in range(count)
    ]
    gather_half(sources, order_ref, level + 1, (1 - upper) * half, [(sent_out, g * TILE) for g in range(count)])


def kept_kernel(level, current, order_ref, kept_out):
    half = order_ref.shape[1] // 2
    sources = [
        (lambda s, g=g: current[g * TILE : (g + 1) * TILE, s * LANES : (s + 1) * LANES]) for g in range(2)
    ]
    gather_half(sources, order_ref, level, upper_half(level) * half, [(kept_out, 0), (kept_out, TILE)])


def last_kernel(swap, kept_ref, got_ref, *refs):
    f_refs, out_ref = refs[:2], refs[2]
    lane = lax.broadcasted_iota(jnp.int32, (8, LANES), 1) // 32
    for k, rhs in joined_blocks(*tiles_of((kept_ref, got_ref), ())):
        rhs = rhs[::-1] if swap else rhs
        out = lax.dot_general(
            block_factors(f_refs, k), jnp.concatenate(rhs * 4, 0), BY_LAST, preferred_element_type=F32
        )
        for e in range(4):
            piece = out[e * 32 : e * 32 + 8]
            for rg in range(1, 4):
                piece = jnp.where(lane == rg, out[e * 32 + rg * 8 : e * 32 + rg * 8 + 8], piece)
            out_ref[4 * k + e] = piece.astype(BF16)


def merge_kernel(same_ref, other_ref, out_ref):
    zhi = lax.axis_index("h")
    slot = lax.broadcasted_iota(jnp.int32, same_ref.shape[1:], 1) // TILE % 2
    for e in range(same_ref.shape[0]):
        same, other = same_ref[e].astype(F32), other_ref[e].astype(F32)
        out_ref[2 * e + zhi] = jnp.where(slot == 0, same, other).astype(BF16)
        out_ref[2 * e + 1 - zhi] = jnp.where(slot == 0, other, same).astype(BF16)


def finish_kernel(in_ref, out_ref, wide):
    count = in_ref.shape[0] // 16
    wide[...] = in_ref[...].astype(F32)
    swap = (lax.axis_index("h") + lax.axis_index("c")) % 2 * TILE
    row = lax.broadcasted_iota(jnp.int32, (LANES, LANES), 0)
    col = lax.broadcasted_iota(jnp.int32, (LANES, LANES), 1)
    flipped = jnp.where(row // TILE % 2 == 0, row + swap, row - swap)
    pick = (flipped == col).astype(BF16)
    left = lax.broadcasted_iota(jnp.int32, (TILE, LANES), 1) < count
    for r8 in range(8):
        by_qh = [wide[pl.ds(qh * 8 + r8, count, stride=16), :] for qh in range(2)]
        straight = jnp.concatenate(by_qh, 0).astype(BF16)
        crossed = jnp.concatenate(by_qh[::-1], 0).astype(BF16)
        straight = lax.dot_general(pick, straight, BY_LAST, preferred_element_type=F32)
        crossed = lax.dot_general(pick, crossed, BY_LAST, preferred_element_type=F32)
        for rg in range(4):
            a = straight[rg * 32 : rg * 32 + 16]
            b = crossed[rg * 32 + 16 : rg * 32 + 32]
            at = (rg * 8 + r8) * 2 * LANES
            for qh, value in enumerate((jnp.where(left, a, b), jnp.where(left, b, a))):
                value = value.astype(BF16)
                lanes = slice(at + qh * LANES, at + (qh + 1) * LANES)
                out_ref[0, :, lanes] = value[:8]
                out_ref[1, :, lanes] = value[8:]


VMEM = pl.BlockSpec(memory_space=pltpu.VMEM)
HBM = pl.BlockSpec(memory_space=pltpu.HBM)


def bf16(*shape):
    return jax.ShapeDtypeStruct(shape, BF16)


def run(name, kernel, operands, outs, scratch=(), space=VMEM, limit=16, flops=1):
    return pl.pallas_call(
        kernel,
        out_shape=outs,
        in_specs=[space] * len(operands),
        out_specs=jax.tree.map(lambda _: VMEM, outs),
        scratch_shapes=scratch,
        compiler_params=pltpu.CompilerParams(vmem_limit_bytes=limit << 20),
        cost_estimate=pl.CostEstimate(flops=flops, bytes_accessed=1, transcendentals=0),
        name=name,
    )(*operands)


def local(probe_vectors, factors, row_orders):
    rows = row_orders.shape[1]
    half = rows // 2
    pts = lax.axis_size("pts")

    def across(value, bit):
        return lax.ppermute(value, "pts", [(i, i ^ 1 << bit) for i in range(pts)])

    def over(value, names):
        count = 2 ** len(names)
        return lax.ppermute(value, names, [(i, count - 1 - i) for i in range(count)])

    near, far, core_near, core_far = run(
        "start", start_kernel, (probe_vectors, row_orders), [bf16(2 * TILE, half)] * 4
    )
    core_far = over(core_far, ("h", "c"))
    core_near = over(core_near, "c")
    near, far, core_near = lax.optimization_barrier((near, far, core_near))
    far = over(far, "h")
    near_got = across(run("near", gather_sent_kernel, (core_near, near), bf16(2 * TILE, half)), 0)
    core_far, factors = lax.optimization_barrier((core_far, factors))
    layers = run(
        "fetch", fetch_kernel, (factors,), [bf16(rows, BLOCK)] * (2 * LEVELS),
        [pltpu.SemaphoreType.DMA((2 * LEVELS,))], HBM, 44,
    )
    far_got = across(run("far", gather_sent_kernel, (core_far, far), bf16(2 * TILE, half)), 0)
    chains = [((core_near, core_far), (near_got, far_got)), ((near, far), (near_got, far_got))]
    for level in range(LEVELS - 1):
        for which in range(2):
            kept, got = chains[which]
            sent, whole = run(
                "level", functools.partial(level_kernel, level, (0, 0, which * TILE, which * TILE)),
                (*kept, *got, *layers[2 * level : 2 * level + 2], row_orders),
                [bf16(2 * TILE, half), bf16(2 * TILE, rows)],
            )
            kept = run(
                "kept", functools.partial(kept_kernel, level + 1), (whole, row_orders), bf16(2 * TILE, half),
                flops=1 << 29,
            )
            kept, waiting = lax.optimization_barrier((kept, chains[1 - which][1]))
            chains[1 - which] = (chains[1 - which][0], waiting)
            chains[which] = ((kept,), (across(sent, level + 1),))
    def last(which, kept, got):
        return run(
            "last", functools.partial(last_kernel, which == 0),
            (*kept, *got, *layers[2 * LEVELS - 2 :]), bf16(pts, 8, LANES),
        )

    other = last(0, *chains[0])
    kept, got = chains[1]
    other, got = lax.optimization_barrier((other, got))
    other = over(other, "c")
    same = last(1, kept, got)
    outgoing = run("merge", merge_kernel, (same, other), bf16(2 * pts, 8, LANES))
    arrived = lax.all_to_all(outgoing, ("pts", "h"), 0, 0, tiled=True)
    return run(
        "finish", finish_kernel, (arrived.reshape(16 * pts, LANES),),
        bf16(2, 8, rows * 4), [pltpu.VMEM((16 * pts, LANES), F32)],
    )


def solution(mesh):
    fine = Mesh(mesh.devices.reshape(mesh.shape["pts"], 2, 2), ("pts", "h", "c"))
    placed = (P(None, ("h", "c"), "pts"), P(None, None, ("pts", "h", "c"), None), P())
    return jax.shard_map(
        local, mesh=fine, in_specs=placed, out_specs=P(None, ("h", "c"), "pts"), check_vma=False
    )
```

```python
import functools

import jax
import jax.numpy as jnp
from jax import lax
from jax.experimental import pallas as pl
from jax.experimental.pallas import tpu as pltpu
from jax.sharding import Mesh
from jax.sharding import PartitionSpec as P

RANK = 64
BLOCK = 2 * RANK
LEVELS = 6
LANES = 128
TILE = 16
BF16 = jnp.bfloat16
F32 = jnp.float32

ALONG_LANES = lax.GatherDimensionNumbers(
    offset_dims=(),
    collapsed_slice_dims=(1,),
    start_index_map=(1,),
    operand_batching_dims=(0,),
    start_indices_batching_dims=(0,),
)
BY_LAST = (((1,), (1,)), ((), ()))


def take_lanes(value, lanes):
    return lax.gather(
        value, lanes[..., None], ALONG_LANES, (1, 1), mode=lax.GatherScatterMode.PROMISE_IN_BOUNDS
    )


def gather_half(sources, order_ref, level, start, targets):
    half = order_ref.shape[1] // 2
    for t in range(half // LANES):
        columns = pl.ds(pl.multiple_of(start + t * LANES, LANES), LANES)
        index = jnp.broadcast_to(order_ref[level : level + 1, columns], (TILE, LANES))
        lane = (index % LANES).astype(jnp.int16)
        which = (index // LANES).astype(jnp.int16)
        picked = [None] * len(sources)
        for s in range(2 * half // LANES):
            here = which == jnp.int16(s)
            for g, source in enumerate(sources):
                value = take_lanes(source(s), lane)
                picked[g] = value if s == 0 else jnp.where(here, value, picked[g])
        for g, (ref, row) in enumerate(targets):
            ref[row : row + TILE, t * LANES : (t + 1) * LANES] = picked[g]


def turned(tile):
    wide = tile.astype(F32)
    return jnp.concatenate([-wide[8:], wide[:8]], 0).astype(BF16)


def joined_blocks(kept, got):
    pairs = [(k, g, turned(k), turned(g)) for k, g in zip(kept, got)]
    for m in range(kept[0].shape[1] // LANES):
        for side in range(2):
            at = slice(m * LANES + side * RANK, m * LANES + (side + 1) * RANK)
            yield 2 * m + side, [
                jnp.concatenate([k[:, at], g[:, at], tk[:, at], tg[:, at]], 1)
                for k, g, tk, tg in pairs
            ]


def block_factors(f_refs, k):
    return jnp.concatenate([ref[k * BLOCK : (k + 1) * BLOCK, :] for ref in f_refs], 1)


def upper_half(bit):
    return lax.axis_index("pts") // (1 << bit) % 2


def fetch_kernel(f_hbm, *refs):
    outs, sems = refs[:-1], refs[-1]
    copies = [
        pltpu.make_async_copy(f_hbm.at[i // 2, i % 2], out, sems.at[i]) for i, out in enumerate(outs)
    ]
    for copy in copies:
        copy.start()
    for copy in copies:
        copy.wait()


def start_kernel(x_ref, order_ref, *outs):
    upper = upper_half(0)
    zhi, core = lax.axis_index("h"), lax.axis_index("c")
    rows = order_ref.shape[1]
    half = rows // 2

    def columns(qh, qc):
        def column(s):
            at = pl.multiple_of((qh * 2 + qc) * rows + s * LANES, LANES)
            return jnp.concatenate(
                [x_ref[0, :, pl.ds(at, LANES)].astype(F32), x_ref[1, :, pl.ds(at, LANES)].astype(F32)], 0
            ).astype(BF16)

        return [column(s) for s in range(rows // LANES)]

    groups = [
        columns(zhi, core), columns(1 - zhi, core), columns(zhi, 1 - core), columns(1 - zhi, 1 - core),
    ]
    sources = [lambda s, g=g: g[s] for g in groups]
    gather_half(sources, order_ref, 0, upper * half, [(out, 0) for out in outs])
    gather_half(sources, order_ref, 0, (1 - upper) * half, [(out, TILE) for out in outs])


def tiles_of(refs, rows):
    if len(refs) == 4:
        tiles = [ref[row : row + TILE, :] for ref, row in zip(refs, rows)]
    else:
        tiles = [ref[row : row + TILE, :] for ref in refs for row in (0, TILE)]
    return tiles[:2], tiles[2:]


def sent_kernel(ref, sent_out):
    sent_out[...] = ref[TILE:, :]


def gather_sent_kernel(core_ref, ref, sent_out):
    sent_out[:TILE, :] = core_ref[TILE:, :]
    sent_out[TILE:, :] = ref[TILE:, :]


def level_kernel(level, at, *refs):
    operands, (*f_refs, order_ref, sent_out, current) = refs[:-5], refs[-5:]
    kept, got = tiles_of(operands, at)
    for k, lhs in joined_blocks(kept, got):
        out = lax.dot_general(
            jnp.concatenate(lhs, 0), block_factors(f_refs, k), BY_LAST, preferred_element_type=F32
        )
        current[:, k * BLOCK : (k + 1) * BLOCK] = out.astype(BF16)
    half = order_ref.shape[1] // 2
    upper = upper_half(level + 1)
    count = len(kept)
    sources = [
        (lambda s, g=g: current[g * TILE : (g + 1) * TILE, s * LANES : (s + 1) * LANES])
        for g in range(count)
    ]
    gather_half(sources, order_ref, level + 1, (1 - upper) * half, [(sent_out, g * TILE) for g in range(count)])


def kept_kernel(level, current, order_ref, kept_out):
    half = order_ref.shape[1] // 2
    sources = [
        (lambda s, g=g: current[g * TILE : (g + 1) * TILE, s * LANES : (s + 1) * LANES]) for g in range(2)
    ]
    gather_half(sources, order_ref, level, upper_half(level) * half, [(kept_out, 0), (kept_out, TILE)])


def last_kernel(swap, kept_ref, got_ref, *refs):
    f_refs, out_ref = refs[:2], refs[2]
    lane = lax.broadcasted_iota(jnp.int32, (8, LANES), 1) // 32
    for k, rhs in joined_blocks(*tiles_of((kept_ref, got_ref), ())):
        rhs = rhs[::-1] if swap else rhs
        out = lax.dot_general(
            block_factors(f_refs, k), jnp.concatenate(rhs * 4, 0), BY_LAST, preferred_element_type=F32
        )
        for e in range(4):
            piece = out[e * 32 : e * 32 + 8]
            for rg in range(1, 4):
                piece = jnp.where(lane == rg, out[e * 32 + rg * 8 : e * 32 + rg * 8 + 8], piece)
            out_ref[4 * k + e] = piece.astype(BF16)


def merge_kernel(same_ref, other_ref, out_ref):
    zhi = lax.axis_index("h")
    slot = lax.broadcasted_iota(jnp.int32, same_ref.shape[1:], 1) // TILE % 2
    for e in range(same_ref.shape[0]):
        same, other = same_ref[e].astype(F32), other_ref[e].astype(F32)
        out_ref[2 * e + zhi] = jnp.where(slot == 0, same, other).astype(BF16)
        out_ref[2 * e + 1 - zhi] = jnp.where(slot == 0, other, same).astype(BF16)


def finish_kernel(in_ref, out_ref, wide):
    count = in_ref.shape[0] // 16
    wide[...] = in_ref[...].astype(F32)
    swap = (lax.axis_index("h") + lax.axis_index("c")) % 2 * TILE
    row = lax.broadcasted_iota(jnp.int32, (LANES, LANES), 0)
    col = lax.broadcasted_iota(jnp.int32, (LANES, LANES), 1)
    flipped = jnp.where(row // TILE % 2 == 0, row + swap, row - swap)
    pick = (flipped == col).astype(BF16)
    left = lax.broadcasted_iota(jnp.int32, (TILE, LANES), 1) < count
    for r8 in range(8):
        by_qh = [wide[pl.ds(qh * 8 + r8, count, stride=16), :] for qh in range(2)]
        straight = jnp.concatenate(by_qh, 0).astype(BF16)
        crossed = jnp.concatenate(by_qh[::-1], 0).astype(BF16)
        straight = lax.dot_general(pick, straight, BY_LAST, preferred_element_type=F32)
        crossed = lax.dot_general(pick, crossed, BY_LAST, preferred_element_type=F32)
        for rg in range(4):
            a = straight[rg * 32 : rg * 32 + 16]
            b = crossed[rg * 32 + 16 : rg * 32 + 32]
            at = (rg * 8 + r8) * 2 * LANES
            for qh, value in enumerate((jnp.where(left, a, b), jnp.where(left, b, a))):
                value = value.astype(BF16)
                lanes = slice(at + qh * LANES, at + (qh + 1) * LANES)
                out_ref[0, :, lanes] = value[:8]
                out_ref[1, :, lanes] = value[8:]


VMEM = pl.BlockSpec(memory_space=pltpu.VMEM)
HBM = pl.BlockSpec(memory_space=pltpu.HBM)


def bf16(*shape):
    return jax.ShapeDtypeStruct(shape, BF16)


def run(name, kernel, operands, outs, scratch=(), space=VMEM, limit=16, flops=1):
    return pl.pallas_call(
        kernel,
        out_shape=outs,
        in_specs=[space] * len(operands),
        out_specs=jax.tree.map(lambda _: VMEM, outs),
        scratch_shapes=scratch,
        compiler_params=pltpu.CompilerParams(vmem_limit_bytes=limit << 20),
        cost_estimate=pl.CostEstimate(flops=flops, bytes_accessed=1, transcendentals=0),
        name=name,
    )(*operands)


def local(probe_vectors, factors, row_orders):
    rows = row_orders.shape[1]
    half = rows // 2
    pts = lax.axis_size("pts")

    def across(value, bit):
        return lax.ppermute(value, "pts", [(i, i ^ 1 << bit) for i in range(pts)])

    def over(value, names):
        count = 2 ** len(names)
        return lax.ppermute(value, names, [(i, count - 1 - i) for i in range(count)])

    near, far, core_near, core_far = run(
        "start", start_kernel, (probe_vectors, row_orders), [bf16(2 * TILE, half)] * 4
    )
    core_far = over(core_far, ("h", "c"))
    core_near = over(core_near, "c")
    near, far, core_near = lax.optimization_barrier((near, far, core_near))
    far = over(far, "h")
    near_got = across(run("near", gather_sent_kernel, (core_near, near), bf16(2 * TILE, half)), 0)
    core_far, factors = lax.optimization_barrier((core_far, factors))
    layers = run(
        "fetch", fetch_kernel, (factors,), [bf16(rows, BLOCK)] * (2 * LEVELS),
        [pltpu.SemaphoreType.DMA((2 * LEVELS,))], HBM, 44,
    )
    core_got = across(run("core_sent", sent_kernel, (core_far,), bf16(TILE, half)), 0)
    far_sent = run("far_sent", sent_kernel, (far,), bf16(TILE, half))
    core_kept, far_sent = lax.optimization_barrier((core_near, far_sent))
    far_got = across(far_sent, 0)
    chains = [((core_kept, core_far), (near_got, core_got)), ((near, far), (near_got, far_got))]
    for level in range(LEVELS - 1):
        for which in range(2):
            kept, got = chains[which]
            sent, whole = run(
                "level", functools.partial(level_kernel, level, (0, 0, which * TILE, 0)),
                (*kept, *got, *layers[2 * level : 2 * level + 2], row_orders),
                [bf16(2 * TILE, half), bf16(2 * TILE, rows)],
            )
            kept = run(
                "kept", functools.partial(kept_kernel, level + 1), (whole, row_orders), bf16(2 * TILE, half),
                flops=1 << 29,
            )
            kept, waiting = lax.optimization_barrier((kept, chains[1 - which][1]))
            chains[1 - which] = (chains[1 - which][0], waiting)
            chains[which] = ((kept,), (across(sent, level + 1),))
    def last(which, kept, got):
        return run(
            "last", functools.partial(last_kernel, which == 0),
            (*kept, *got, *layers[2 * LEVELS - 2 :]), bf16(pts, 8, LANES),
        )

    other = last(0, *chains[0])
    kept, got = chains[1]
    other, got = lax.optimization_barrier((other, got))
    other = over(other, "c")
    same = last(1, kept, got)
    outgoing = run("merge", merge_kernel, (same, other), bf16(2 * pts, 8, LANES))
    arrived = lax.all_to_all(outgoing, ("pts", "h"), 0, 0, tiled=True)
    return run(
        "finish", finish_kernel, (arrived.reshape(16 * pts, LANES),),
        bf16(2, 8, rows * 4), [pltpu.VMEM((16 * pts, LANES), F32)],
    )


def solution(mesh):
    fine = Mesh(mesh.devices.reshape(mesh.shape["pts"], 2, 2), ("pts", "h", "c"))
    placed = (P(None, ("h", "c"), "pts"), P(None, None, ("pts", "h", "c"), None), P())
    return jax.shard_map(
        local, mesh=fine, in_specs=placed, out_specs=P(None, ("h", "c"), "pts"), check_vma=False
    )
```

```python
import functools

import jax
import jax.numpy as jnp
from jax import lax
from jax.experimental import pallas as pl
from jax.experimental.pallas import tpu as pltpu
from jax.sharding import Mesh
from jax.sharding import PartitionSpec as P

RANK = 64
BLOCK = 2 * RANK
LEVELS = 6
LANES = 128
TILE = 16
BF16 = jnp.bfloat16
F32 = jnp.float32

ALONG_LANES = lax.GatherDimensionNumbers(
    offset_dims=(),
    collapsed_slice_dims=(1,),
    start_index_map=(1,),
    operand_batching_dims=(0,),
    start_indices_batching_dims=(0,),
)
BY_LAST = (((1,), (1,)), ((), ()))


def take_lanes(value, lanes):
    return lax.gather(
        value, lanes[..., None], ALONG_LANES, (1, 1), mode=lax.GatherScatterMode.PROMISE_IN_BOUNDS
    )


def gather_columns(sources, index, count):
    lane = (index % LANES).astype(jnp.int16)
    which = (index // LANES).astype(jnp.int16)
    picked = [None] * len(sources)
    for s in range(count):
        here = which == jnp.int16(s)
        for g, source in enumerate(sources):
            value = take_lanes(source(s), lane)
            picked[g] = value if s == 0 else jnp.where(here, value, picked[g])
    return picked


def gather_half(sources, order_ref, level, start, targets):
    half = order_ref.shape[1] // 2
    for t in range(half // LANES):
        columns = pl.ds(pl.multiple_of(start + t * LANES, LANES), LANES)
        index = jnp.broadcast_to(order_ref[level : level + 1, columns], (TILE, LANES))
        values = gather_columns(sources, index, 2 * half // LANES)
        for (ref, row), value in zip(targets, values):
            ref[row : row + TILE, t * LANES : (t + 1) * LANES] = value


def turned(tile):
    wide = tile.astype(F32)
    return jnp.concatenate([-wide[8:], wide[:8]], 0).astype(BF16)


def joined_blocks(kept, got):
    pairs = [(k, g, turned(k), turned(g)) for k, g in zip(kept, got)]
    for m in range(kept[0].shape[1] // LANES):
        for side in range(2):
            at = slice(m * LANES + side * RANK, m * LANES + (side + 1) * RANK)
            yield 2 * m + side, [
                jnp.concatenate([k[:, at], g[:, at], tk[:, at], tg[:, at]], 1)
                for k, g, tk, tg in pairs
            ]


def block_factors(f_refs, k):
    return jnp.concatenate([ref[k * BLOCK : (k + 1) * BLOCK, :] for ref in f_refs], 1)


def upper_half(bit):
    return lax.axis_index("pts") // (1 << bit) % 2


def fetch_kernel(f_hbm, *refs):
    outs, sems = refs[:-1], refs[-1]
    copies = [
        pltpu.make_async_copy(f_hbm.at[i // 2, i % 2], out, sems.at[i]) for i, out in enumerate(outs)
    ]
    for copy in copies:
        copy.start()
    for copy in copies:
        copy.wait()


def side_kernel(side_out):
    side_out[...] = jnp.full(side_out.shape, upper_half(0), jnp.int32)


def start_kernel(x_ref, order_ref, side_ref, *outs):
    zhi, core = lax.axis_index("h"), lax.axis_index("c")
    rows = order_ref.shape[1]
    half = rows // 2

    def columns(qh, qc):
        def column(s):
            at = pl.multiple_of((qh * 2 + qc) * rows + s * LANES, LANES)
            return jnp.concatenate(
                [x_ref[0, :, pl.ds(at, LANES)].astype(F32), x_ref[1, :, pl.ds(at, LANES)].astype(F32)], 0
            ).astype(BF16)

        return [column(s) for s in range(rows // LANES)]

    groups = [
        columns(zhi, core), columns(1 - zhi, core), columns(zhi, 1 - core), columns(1 - zhi, 1 - core),
    ]
    sources = [lambda s, g=g: g[s] for g in groups]
    upper = side_ref[...] == 1
    for t in range(half // LANES):
        low, high = (
            jnp.broadcast_to(order_ref[0:1, at : at + LANES], (TILE, LANES)) for at in (t * LANES, half + t * LANES)
        )
        for row, index in ((0, jnp.where(upper, high, low)), (TILE, jnp.where(upper, low, high))):
            for out, value in zip(outs, gather_columns(sources, index, rows // LANES)):
                out[row : row + TILE, t * LANES : (t + 1) * LANES] = value


def tiles_of(refs, rows):
    if len(refs) == 4:
        tiles = [ref[row : row + TILE, :] for ref, row in zip(refs, rows)]
    else:
        tiles = [ref[row : row + TILE, :] for ref in refs for row in (0, TILE)]
    return tiles[:2], tiles[2:]


def sent_kernel(ref, sent_out):
    sent_out[...] = ref[TILE:, :]


def gather_sent_kernel(core_ref, ref, sent_out):
    sent_out[:TILE, :] = core_ref[TILE:, :]
    sent_out[TILE:, :] = ref[TILE:, :]


def level_kernel(level, at, *refs):
    operands, (*f_refs, order_ref, sent_out, current) = refs[:-5], refs[-5:]
    kept, got = tiles_of(operands, at)
    for k, lhs in joined_blocks(kept, got):
        out = lax.dot_general(
            jnp.concatenate(lhs, 0), block_factors(f_refs, k), BY_LAST, preferred_element_type=F32
        )
        current[:, k * BLOCK : (k + 1) * BLOCK] = out.astype(BF16)
    half = order_ref.shape[1] // 2
    upper = upper_half(level + 1)
    count = len(kept)
    sources = [
        (lambda s, g=g: current[g * TILE : (g + 1) * TILE, s * LANES : (s + 1) * LANES])
        for g in range(count)
    ]
    gather_half(sources, order_ref, level + 1, (1 - upper) * half, [(sent_out, g * TILE) for g in range(count)])


def kept_kernel(level, current, order_ref, kept_out):
    half = order_ref.shape[1] // 2
    sources = [
        (lambda s, g=g: current[g * TILE : (g + 1) * TILE, s * LANES : (s + 1) * LANES]) for g in range(2)
    ]
    gather_half(sources, order_ref, level, upper_half(level) * half, [(kept_out, 0), (kept_out, TILE)])


def last_kernel(swap, kept_ref, got_ref, *refs):
    f_refs, out_ref = refs[:2], refs[2]
    lane = lax.broadcasted_iota(jnp.int32, (8, LANES), 1) // 32
    for k, rhs in joined_blocks(*tiles_of((kept_ref, got_ref), ())):
        rhs = rhs[::-1] if swap else rhs
        out = lax.dot_general(
            block_factors(f_refs, k), jnp.concatenate(rhs * 4, 0), BY_LAST, preferred_element_type=F32
        )
        for e in range(4):
            piece = out[e * 32 : e * 32 + 8]
            for rg in range(1, 4):
                piece = jnp.where(lane == rg, out[e * 32 + rg * 8 : e * 32 + rg * 8 + 8], piece)
            out_ref[4 * k + e] = piece.astype(BF16)


def merge_kernel(same_ref, other_ref, out_ref):
    zhi = lax.axis_index("h")
    slot = lax.broadcasted_iota(jnp.int32, same_ref.shape[1:], 1) // TILE % 2
    for e in range(same_ref.shape[0]):
        same, other = same_ref[e].astype(F32), other_ref[e].astype(F32)
        out_ref[2 * e + zhi] = jnp.where(slot == 0, same, other).astype(BF16)
        out_ref[2 * e + 1 - zhi] = jnp.where(slot == 0, other, same).astype(BF16)


def finish_kernel(in_ref, out_ref, wide):
    count = in_ref.shape[0] // 16
    wide[...] = in_ref[...].astype(F32)
    swap = (lax.axis_index("h") + lax.axis_index("c")) % 2 * TILE
    row = lax.broadcasted_iota(jnp.int32, (LANES, LANES), 0)
    col = lax.broadcasted_iota(jnp.int32, (LANES, LANES), 1)
    flipped = jnp.where(row // TILE % 2 == 0, row + swap, row - swap)
    pick = (flipped == col).astype(BF16)
    left = lax.broadcasted_iota(jnp.int32, (TILE, LANES), 1) < count
    for r8 in range(8):
        by_qh = [wide[pl.ds(qh * 8 + r8, count, stride=16), :] for qh in range(2)]
        straight = jnp.concatenate(by_qh, 0).astype(BF16)
        crossed = jnp.concatenate(by_qh[::-1], 0).astype(BF16)
        straight = lax.dot_general(pick, straight, BY_LAST, preferred_element_type=F32)
        crossed = lax.dot_general(pick, crossed, BY_LAST, preferred_element_type=F32)
        for rg in range(4):
            a = straight[rg * 32 : rg * 32 + 16]
            b = crossed[rg * 32 + 16 : rg * 32 + 32]
            at = (rg * 8 + r8) * 2 * LANES
            for qh, value in enumerate((jnp.where(left, a, b), jnp.where(left, b, a))):
                value = value.astype(BF16)
                lanes = slice(at + qh * LANES, at + (qh + 1) * LANES)
                out_ref[0, :, lanes] = value[:8]
                out_ref[1, :, lanes] = value[8:]


VMEM = pl.BlockSpec(memory_space=pltpu.VMEM)
HBM = pl.BlockSpec(memory_space=pltpu.HBM)


def bf16(*shape):
    return jax.ShapeDtypeStruct(shape, BF16)


def run(name, kernel, operands, outs, scratch=(), space=VMEM, limit=16, flops=1):
    return pl.pallas_call(
        kernel,
        out_shape=outs,
        in_specs=[space] * len(operands),
        out_specs=jax.tree.map(lambda _: VMEM, outs),
        scratch_shapes=scratch,
        compiler_params=pltpu.CompilerParams(vmem_limit_bytes=limit << 20),
        cost_estimate=pl.CostEstimate(flops=flops, bytes_accessed=1, transcendentals=0),
        name=name,
    )(*operands)


def local(probe_vectors, factors, row_orders):
    rows = row_orders.shape[1]
    half = rows // 2
    pts = lax.axis_size("pts")

    def across(value, bit):
        return lax.ppermute(value, "pts", [(i, i ^ 1 << bit) for i in range(pts)])

    def over(value, names):
        count = 2 ** len(names)
        return lax.ppermute(value, names, [(i, count - 1 - i) for i in range(count)])

    side = run("side", side_kernel, (), jax.ShapeDtypeStruct((TILE, LANES), jnp.int32), flops=1 << 33)
    near, far, core_near, core_far = run(
        "start", start_kernel, (probe_vectors, row_orders, side), [bf16(2 * TILE, half)] * 4
    )
    core_far = over(core_far, ("h", "c"))
    core_near = over(core_near, "c")
    near, far, core_near = lax.optimization_barrier((near, far, core_near))
    far = over(far, "h")
    near_got = across(run("near", gather_sent_kernel, (core_near, near), bf16(2 * TILE, half)), 0)
    core_far, factors = lax.optimization_barrier((core_far, factors))
    layers = run(
        "fetch", fetch_kernel, (factors,), [bf16(rows, BLOCK)] * (2 * LEVELS),
        [pltpu.SemaphoreType.DMA((2 * LEVELS,))], HBM, 44,
    )
    core_got = across(run("core_sent", sent_kernel, (core_far,), bf16(TILE, half)), 0)
    far_sent = run("far_sent", sent_kernel, (far,), bf16(TILE, half))
    core_kept, far_sent = lax.optimization_barrier((core_near, far_sent))
    far_got = across(far_sent, 0)
    chains = [((core_kept, core_far), (near_got, core_got)), ((near, far), (near_got, far_got))]
    for level in range(LEVELS - 1):
        for which in range(2):
            kept, got = chains[which]
            sent, whole = run(
                "level", functools.partial(level_kernel, level, (0, 0, which * TILE, 0)),
                (*kept, *got, *layers[2 * level : 2 * level + 2], row_orders),
                [bf16(2 * TILE, half), bf16(2 * TILE, rows)],
            )
            kept = run(
                "kept", functools.partial(kept_kernel, level + 1), (whole, row_orders), bf16(2 * TILE, half),
                flops=1 << 29,
            )
            kept, waiting = lax.optimization_barrier((kept, chains[1 - which][1]))
            chains[1 - which] = (chains[1 - which][0], waiting)
            chains[which] = ((kept,), (across(sent, level + 1),))
    def last(which, kept, got):
        return run(
            "last", functools.partial(last_kernel, which == 0),
            (*kept, *got, *layers[2 * LEVELS - 2 :]), bf16(pts, 8, LANES), flops=1 << 33,
        )

    other = last(0, *chains[0])
    other = over(other, "c")
    same = last(1, *chains[1])
    outgoing = run("merge", merge_kernel, (same, other), bf16(2 * pts, 8, LANES))
    arrived = lax.all_to_all(outgoing, ("pts", "h"), 0, 0, tiled=True)
    return run(
        "finish", finish_kernel, (arrived.reshape(16 * pts, LANES),),
        bf16(2, 8, rows * 4), [pltpu.VMEM((16 * pts, LANES), F32)],
    )


def solution(mesh):
    fine = Mesh(mesh.devices.reshape(mesh.shape["pts"], 2, 2), ("pts", "h", "c"))
    placed = (P(None, ("h", "c"), "pts"), P(None, None, ("pts", "h", "c"), None), P())
    return jax.shard_map(
        local, mesh=fine, in_specs=placed, out_specs=P(None, ("h", "c"), "pts"), check_vma=False
    )
```
